768 devices in a mesh: row: 128 (over x, y, z_hi, core), col: 6 (over z_lo).
Axes of the slice: x: 4, y: 8, z: 12 (z_hi: 2, z_lo: 6; z = z_hi * 6 + z_lo), core: 2. Of those that a mesh axis runs over, the one named last changes fastest.
Arguments:
- vectors: float32 [8, 9437184], P(None, ('row', 'col')), may hold values from -6 to 6
- tiles: bfloat16 [49152, 128, 128], P(('row', 'col')), may hold values from -0.25 to 0.25
- tile_rows: int32 [49152], P(('row', 'col')), may hold values from 0 to 73727, as said below
- tile_cols: int32 [49152], P(('row', 'col')), may hold values from 0 to 73727, as said below
- row_counts: int32 [49152], P(('row', 'col')), may hold values from 1 to 128, as said below
- live_tiles: int32 [768], P(('row', 'col')), may hold values from 1 to 64, as said below
Outputs:
- product: float32 [8, 9437184], P(None, ('row', 'col'))
The draws below stay inside these ranges and needn't reach their ends.
Inputs may be any that keep to these rules, and one draw needn't show every extreme that they name: `tile_rows`: A slot of device d (row index rr, col index cc) has a tile row in its row band, rr * 6 * 96 up to (rr + 1) * 6 * 96 - 1; a slot beyond the device's live count repeats the coordinates of the device's first slot. `tile_cols`: A slot's tile column j satisfies (j // 96) % 6 == cc, j // 576 lies between rr and rr + 6, and j >= its tile row; places may repeat. `row_counts`: slot 0 of every device has 128 rows. `live_tiles`: live slots are the first of each device; device 0 has all 64 live.
All inputs are finite; a program needn't handle non-finite values.
Results may differ from the reference program's by a relative error of at most 0.0029.
Values may be sent and summed in bfloat16 or wider, within the bound.
No kernel may reach another device: no remote copies, remote signals or barrier semaphores. Data moves between devices by JAX's collectives and lax.ppermute only.
A program may use at most 32 MiB of HBM per device.

```python
import jax
import jax.numpy as jnp
from jax import lax

NVEC = 8
TILE = 128
TILES_PIECE = 96
REACH = 6
TILE_SLOTS = 64
NSTATES = 9437184
NTILES = 73728
N_ROW = 128
N_COL = 6


def tile_layout(key):
    device_count = N_ROW * N_COL
    band_rows = N_COL * TILES_PIECE
    devices = jnp.arange(device_count, dtype=jnp.int32)
    row_place = devices // N_COL
    col_place = devices % N_COL
    reach_here = jnp.minimum(REACH, N_ROW - 1 - row_place)
    band_step = jax.random.randint(jax.random.fold_in(key, 101), (device_count, TILE_SLOTS), 0, reach_here[:, None] + 1)
    position = jax.random.randint(jax.random.fold_in(key, 102), (device_count, TILE_SLOTS), 0, TILES_PIECE)
    cols = ((row_place[:, None] + band_step) * N_COL + col_place[:, None]) * TILES_PIECE + position
    row_limit = jnp.where(band_step == 0, col_place[:, None] * TILES_PIECE + position + 1, band_rows)
    offsets = jax.random.randint(jax.random.fold_in(key, 103), (device_count, TILE_SLOTS), 0, row_limit)
    rows = row_place[:, None] * band_rows + offsets
    target = jax.random.randint(jax.random.fold_in(key, 104), (device_count,), max(1, TILE_SLOTS // 8), TILE_SLOTS + 1)
    live = jnp.where(devices == 0, TILE_SLOTS, target).astype(jnp.int32)
    slot_ids = jnp.arange(TILE_SLOTS, dtype=jnp.int32)
    in_use = slot_ids[None, :] < live[:, None]
    rows = jnp.where(in_use, rows, rows[:, :1])
    cols = jnp.where(in_use, cols, cols[:, :1])
    return (rows.reshape(-1).astype(jnp.int32), cols.reshape(-1).astype(jnp.int32), live)


def draw_tile_rows(key, part):
    return tile_layout(key)[0]


def draw_tile_cols(key, part):
    return tile_layout(key)[1]


def draw_live_tiles(key, part):
    return tile_layout(key)[2]


def draw_row_counts(key, part):
    key = jax.random.fold_in(key, 7)
    counts = jax.random.randint(key, (N_ROW * N_COL, TILE_SLOTS), 1, TILE + 1)
    counts = counts.at[:, 0].set(TILE)
    return counts.reshape(-1).astype(jnp.int32)


def level_of(rng, shape, pieces, least, high):
    gain, own = 1.0, jax.random.fold_in(rng, 6)
    for dim, shards_of in pieces:
        steps = jnp.exp(jax.random.uniform(jax.random.fold_in(own, dim), (shards_of,), jnp.float32, least / len(pieces), high / len(pieces)))
        gain = gain * jnp.repeat(steps, shape[dim] // shards_of).reshape([-1 if axis == dim else 1 for axis in range(len(shape))])
    return gain


def normal_values(own_key, shape, spread, bound, pieces=(), kind=jnp.bfloat16):
    drawn = jax.random.normal(own_key, shape, jnp.float32) * spread
    if len(pieces) > 0:
        drawn = level_of(own_key, shape, pieces, -0.22, 0.18) * drawn
    return jnp.clip(drawn, min=-bound, max=bound).astype(kind)


def setup_inputs(seed: int = 0) -> dict:
    key_of = jax.random.split(jax.random.key(seed), 7)
    return {
        "vectors": normal_values(key_of[0], (NVEC, NSTATES), 1.0, 6.0, ((1, 768),), jnp.float32),
        "tiles": normal_values(key_of[1], (N_ROW * N_COL * TILE_SLOTS, TILE, TILE), (4 * TILE) ** -0.5, 0.25, ((0, 768),)),
        "tile_rows": draw_tile_rows(jax.random.fold_in(key_of[6], 71), 0),
        "tile_cols": draw_tile_cols(jax.random.fold_in(key_of[6], 71), 0),
        "row_counts": draw_row_counts(jax.random.fold_in(key_of[6], 71), 0),
        "live_tiles": draw_live_tiles(jax.random.fold_in(key_of[6], 71), 0),
    }


def reference(vectors, tiles, tile_rows, tile_cols, row_counts, live_tiles):
    device_count = N_ROW * N_COL
    rounded = lax.optimization_barrier(vectors.astype(jnp.bfloat16)).astype(jnp.float32)
    columns = rounded.reshape(NVEC, NTILES, TILE)
    lane_ids = jnp.arange(TILE, dtype=jnp.int32)
    slot_ids = jnp.arange(TILE_SLOTS, dtype=jnp.int32)

    def apply_device(accumulated, scanned):
        block, row_ids, col_ids, counts, live_count = scanned
        counts = jnp.where(slot_ids < live_count, counts, 0)
        row_mask = (lane_ids[None, :] < counts[:, None]).astype(jnp.float32)
        tile_wide = block.astype(jnp.float32)
        forward = jnp.einsum("tik,btk->bti", tile_wide, columns[:, col_ids]) * row_mask[None]
        accumulated = accumulated.at[:, row_ids].add(forward)
        mirror = jnp.einsum("tik,bti->btk", tile_wide, columns[:, row_ids] * row_mask[None])
        accumulated = accumulated.at[:, col_ids].add(mirror)
        return accumulated, None

    scanned = (tiles.reshape(device_count, TILE_SLOTS, TILE, TILE),
               tile_rows.reshape(device_count, TILE_SLOTS),
               tile_cols.reshape(device_count, TILE_SLOTS),
               row_counts.reshape(device_count, TILE_SLOTS),
               live_tiles)
    accumulated, _ = lax.scan(apply_device, jnp.zeros((NVEC, NTILES, TILE), jnp.float32), scanned)
    return accumulated.reshape(NVEC, NSTATES)
```

```python
import functools

import jax
import jax.numpy as jnp
from jax import lax
from jax.experimental import pallas as pl
from jax.experimental.pallas import tpu as pltpu
from jax.sharding import PartitionSpec as P

AXES = ("row", "col")
VMEM_BYTES = 40 * 1024 * 1024
LIST_TAIL = 16


def whole(count):
    return [pl.BlockSpec(memory_space=pltpu.VMEM)] * count


def send(value, moves):
    return lax.ppermute(value, AXES, moves)


def moves_of(rows, cols, target):
    pairs = []
    for row in range(rows):
        for col in range(cols):
            to = target(row, col)
            if to is not None and 0 <= to[0] < rows:
                pairs.append((row * cols + col, to[0] * cols + to[1]))
    return pairs


def across_columns(value, rows, cols):
    half = cols // 2
    far = send(value, moves_of(rows, cols, lambda r, c: (r, (c + half) % cols)))
    pair = jnp.concatenate([value, far], axis=0)
    parts = [pair]
    for step in (1, 2):
        parts.append(
            send(pair, moves_of(rows, cols, lambda r, c, s=step: (r, c // half * half + (c % half + s) % half)))
        )
    return parts


def along_rows(value, rows, cols, way):
    last_half = 1 if way < 0 else 0
    across = send(value, moves_of(rows, cols, lambda r, c: (r ^ 2, c)))
    both = jnp.concatenate([value, across], axis=0)
    next_group = send(both, moves_of(rows, cols, lambda r, c: (r + 4 * way, c)))
    far_group = send(
        across,
        moves_of(rows, cols, lambda r, c: (r + 8 * way, c) if r // 2 % 2 == last_half else None),
    )
    here = jnp.concatenate([both, next_group, far_group], axis=0)
    there = send(here, moves_of(rows, cols, lambda r, c: (r ^ 1, c)))
    return [here, there]


def product_kernel(forward, parts, places_ref, counts_ref, *refs):
    pieces, (tiles_ref, tail_ref, out_ref, wide, sums) = refs[:parts], refs[parts:]
    start = 0
    for piece in pieces:
        wide[start : start + piece.shape[0], :] = piece[...].astype(jnp.float32)
        start += piece.shape[0]
    slots = tiles_ref.shape[0]
    lanes = lax.broadcasted_iota(jnp.int32, (8, 128), 1)
    for slot in range(slots):
        place = pl.multiple_of(places_ref[slot] * 8, 8)
        mask = lanes < counts_ref[slot]
        x = wide[pl.ds(place, 8), :]
        if forward:
            y = lax.dot_general(
                x.astype(jnp.bfloat16), tiles_ref[slot], (((1,), (1,)), ((), ())), preferred_element_type=jnp.float32
            )
            y = jnp.where(mask, y, 0.0)
        else:
            x = jnp.where(mask, x, 0.0).astype(jnp.bfloat16)
            y = lax.dot_general(x, tiles_ref[slot], (((1,), (0,)), ((), ())), preferred_element_type=jnp.float32)
        sums[pl.ds(slot, 8, stride=slots), :] = y
    out_ref[: 8 * slots, :] = sums[...].astype(jnp.bfloat16)
    out_ref[8 * slots :, :] = tail_ref[...]


def products(forward, parts, places, counts, tiles, tail):
    slots = tiles.shape[0]
    total = sum(p.shape[0] for p in parts)
    return pl.pallas_call(
        functools.partial(product_kernel, forward, len(parts)),
        out_shape=jax.ShapeDtypeStruct((8 * slots + LIST_TAIL, 128), jnp.bfloat16),
        in_specs=[pl.BlockSpec(memory_space=pltpu.SMEM)] * 2 + whole(len(parts) + 2),
        out_specs=pl.BlockSpec(memory_space=pltpu.VMEM),
        scratch_shapes=[pltpu.VMEM((total, 128), jnp.float32), pltpu.VMEM((8 * slots, 128), jnp.float32)],
        compiler_params=pltpu.CompilerParams(vmem_limit_bytes=VMEM_BYTES),
        cost_estimate=pl.CostEstimate(flops=2 * 8 * 128 * 128 * slots, bytes_accessed=total * 256 + 2 * 2**20, transcendentals=0),
    )(places, counts, *parts, tiles, tail)


def sum_kernel(parts, slots, base_ref, *refs):
    lists, (out_ref, acc) = refs[:parts], refs[parts:]
    tiles_here = out_ref.shape[0] // 8
    rows = 8 * slots + LIST_TAIL
    own = lax.broadcasted_iota(jnp.int32, (tiles_here, 128), 0) + base_ref[0]
    own = own.astype(jnp.float32)
    acc[...] = jnp.zeros_like(acc)
    for part in lists:
        for start in range(0, part.shape[0], rows):
            digits = part[start + 8 * slots : start + rows, :].astype(jnp.float32)
            ids = digits[0:1] + 64.0 * digits[1:2] + 4096.0 * digits[2:3]
            chosen = jnp.where(own == ids, 1.0, 0.0)[:, :slots].astype(jnp.bfloat16)
            for vec in range(8):
                values = part[start + vec * slots : start + (vec + 1) * slots, :]
                acc[vec] += jnp.dot(chosen, values, preferred_element_type=jnp.float32)
    for vec in range(8):
        out_ref[pl.ds(vec, tiles_here, stride=8), :] = acc[vec]


def summed(lists, slots, base, tiles_here):
    return pl.pallas_call(
        functools.partial(sum_kernel, len(lists), slots),
        out_shape=jax.ShapeDtypeStruct((8 * tiles_here, 128), jnp.float32),
        in_specs=[pl.BlockSpec(memory_space=pltpu.SMEM)] + whole(len(lists)),
        out_specs=pl.BlockSpec(memory_space=pltpu.VMEM),
        scratch_shapes=[pltpu.VMEM((8, tiles_here, 128), jnp.float32)],
        compiler_params=pltpu.CompilerParams(vmem_limit_bytes=VMEM_BYTES),
    )(base, *lists)


def tail_of(ids):
    digits = jnp.stack([jnp.where(ids < 0, ids, ids % 64), jnp.maximum(ids, 0) // 64 % 64, jnp.maximum(ids, 0) // 4096])
    return jnp.pad(digits.astype(jnp.bfloat16), ((0, LIST_TAIL - 3), (0, 128 - ids.shape[0])))


def local(vectors, tiles, tile_rows, tile_cols, row_counts, live_tiles):
    vec_count, seg_len = vectors.shape
    slots, tile_len = tiles.shape[:2]
    rows, cols = lax.axis_size("row"), lax.axis_size("col")
    half = cols // 2
    per_piece = seg_len // tile_len
    band = cols * per_piece
    row, col = lax.axis_index("row"), lax.axis_index("col")

    live = jnp.arange(slots, dtype=jnp.int32) < live_tiles[0]
    counts = jnp.where(live, row_counts, 0)
    row_piece = tile_rows // per_piece % cols
    row_part = (col % half - row_piece % half) % half * 2 + jnp.where(row_piece // half != col // half, 1, 0)
    row_places = row_part * per_piece + tile_rows % per_piece
    col_row = tile_cols // band
    group = col_row // 4 - row // 4
    other = (col_row % 4) ^ (row % 4)
    col_part = (other & 1) * 5 + jnp.where(group == 2, 4, (other >> 1) + 2 * group)
    col_places = col_part * per_piece + tile_cols % per_piece

    def flat(x):
        return x.reshape(vec_count, per_piece, tile_len).transpose(1, 0, 2).reshape(-1, tile_len)

    rounded = flat(vectors.astype(jnp.bfloat16))
    row_parts = across_columns(rounded, rows, cols)
    col_parts = along_rows(rounded, rows, cols, -1)
    mirror = products(False, row_parts, row_places, counts, tiles, tail_of(jnp.where(live, tile_cols, -1)))
    forward = products(True, col_parts, col_places, counts, tiles, tail_of(jnp.where(live, tile_rows, -1)))
    mirror_lists = along_rows(mirror, rows, cols, 1)
    forward_lists = across_columns(forward, rows, cols)
    base = ((row * cols + col) * per_piece).reshape(1)
    total = summed(mirror_lists + forward_lists, slots, base, per_piece)
    return total.reshape(per_piece, vec_count, tile_len).transpose(1, 0, 2).reshape(vec_count, seg_len)


def solution(mesh):
    placed = (
        P(None, AXES),
        P(AXES, None, None),
        P(AXES),
        P(AXES),
        P(AXES),
        P(AXES),
    )
    return jax.shard_map(local, mesh=mesh, in_specs=placed, out_specs=P(None, AXES), check_vma=False)
```

```python
import functools

import jax
import jax.numpy as jnp
from jax import lax
from jax.experimental import pallas as pl
from jax.experimental.pallas import tpu as pltpu
from jax.sharding import PartitionSpec as P

AXES = ("row", "col")
VMEM_BYTES = 40 * 1024 * 1024
LIST_TAIL = 16
SHARE = 32
LANES = 128
VMEM = pl.BlockSpec(memory_space=pltpu.VMEM)
SMEM = pl.BlockSpec(memory_space=pltpu.SMEM)
PARAMS = pltpu.CompilerParams(vmem_limit_bytes=VMEM_BYTES)
LITTLE = pl.CostEstimate(flops=0, bytes_accessed=0, transcendentals=0)


def send(value, moves):
    return lax.ppermute(value, AXES, moves)


def moves_of(rows, cols, target):
    pairs = []
    for row in range(rows):
        for col in range(cols):
            to = target(row, col)
            if to is not None and 0 <= to[0] < rows:
                pairs.append((row * cols + col, to[0] * cols + to[1]))
    return pairs


def across_halves(value, rows, cols):
    return send(value, moves_of(rows, cols, lambda r, c: (r ^ 2, c)))


def next_groups(both, rows, cols, way):
    last_half = 1 if way < 0 else 0
    count = both.shape[0] // 2
    return [
        send(both, moves_of(rows, cols, lambda r, c: (r + 4 * way, c))),
        send(
            both[count:],
            moves_of(rows, cols, lambda r, c: (r + 8 * way, c) if r // 2 % 2 == last_half else None),
        ),
    ]


def other_core(here, rows, cols):
    return send(here, moves_of(rows, cols, lambda r, c: (r ^ 1, c)))


def over_columns(value, cols):
    return lax.all_to_all(value.reshape(cols, -1, LANES), "col", 0, 0).reshape(-1, LANES)


def after(value, *others):
    return lax.optimization_barrier((value, *others))[0]


def request_kernel(cols, per_piece, place_ref, rows_ref, live_ref, ids_ref, places_ref, used):
    slots = rows_ref.shape[0]
    me, start = place_ref[0], place_ref[1]
    for col in range(cols):
        used[col] = 0
    live = live_ref[0]
    for slot in range(slots):
        tile = rows_ref[slot] - start
        col = jnp.int32(0)
        for edge in range(1, cols):
            col = col + jnp.where(tile >= edge * per_piece, 1, 0)
        here = slot < live
        rank = used[col]
        used[col] = rank + jnp.where(here, 1, 0)
        ids_ref[col, 0, rank] = tile - col * per_piece
        late = jnp.where(rank < SHARE, 0, 1)
        chunk = jnp.where(col == me, 2 * cols + late, col + cols * late)
        places_ref[slot] = jnp.where(here, chunk * (8 * SHARE) + rank - late * SHARE, (2 * cols + 2) * 8 * SHARE)
    most = jnp.int32(0)
    for col in range(cols):
        most = jnp.maximum(most, jnp.where(col == me, 0, used[col]))
    for col in range(cols):
        ids_ref[col, 1, 0] = most
        ids_ref[col, 1, 1] = used[col]


def requests(place, tile_rows, live_tiles, cols, per_piece):
    slots = tile_rows.shape[0]
    return pl.pallas_call(
        functools.partial(request_kernel, cols, per_piece),
        out_shape=(
            jax.ShapeDtypeStruct((cols, 8, LANES), jnp.int32),
            jax.ShapeDtypeStruct((slots,), jnp.int32),
        ),
        in_specs=[SMEM, SMEM, SMEM],
        out_specs=(SMEM, SMEM),
        scratch_shapes=[pltpu.SMEM((cols,), jnp.int32)],
        cost_estimate=LITTLE,
    )(place, tile_rows, live_tiles)


def chosen_of(asked_ref, col, places):
    lanes = lax.broadcasted_iota(jnp.int32, places.shape, 1)
    asked = (places == asked_ref[col, 0:1, :]) & (lanes < asked_ref[col, 1:2, 1:2])
    return jnp.where(asked, 1.0, 0.0)


def reply_kernel(cols, slots, place_ref, asked_ref, x_ref, first_ref, second_ref, own_ref, wide):
    tiles = x_ref.shape[0] // 8
    wide[...] = x_ref[...].astype(jnp.float32)
    places = lax.broadcasted_iota(jnp.int32, (LANES, LANES), 0)
    wanted = [chosen_of(asked_ref, col, places).T[:slots, :tiles] for col in [*range(cols), place_ref[0]]]
    wanted = jnp.concatenate(wanted, axis=0).astype(jnp.bfloat16)
    for vec in range(8):
        x = wide[pl.ds(vec, tiles, stride=8), :].astype(jnp.bfloat16)
        found = jnp.dot(wanted, x, preferred_element_type=jnp.float32).astype(jnp.bfloat16)
        for col in range(cols + 1):
            early = found[col * slots : col * slots + SHARE]
            late = found[col * slots + SHARE : (col + 1) * slots]
            at = (col * 8 + vec) * SHARE
            if col < cols:
                first_ref[at : at + SHARE, :] = early
                second_ref[at : at + SHARE, :] = late
            else:
                own_ref[vec * SHARE : (vec + 1) * SHARE, :] = early
                own_ref[(8 + vec) * SHARE : (9 + vec) * SHARE, :] = late


def replies(place, asked, x, cols, slots):
    shape = jax.ShapeDtypeStruct((cols * 8 * SHARE, LANES), jnp.bfloat16)
    own = jax.ShapeDtypeStruct((2 * 8 * SHARE, LANES), jnp.bfloat16)
    return pl.pallas_call(
        functools.partial(reply_kernel, cols, slots),
        out_shape=(shape, shape, own),
        in_specs=[SMEM, VMEM, VMEM],
        out_specs=(VMEM, VMEM, VMEM),
        scratch_shapes=[pltpu.VMEM(x.shape, jnp.float32)],
        compiler_params=PARAMS,
        cost_estimate=LITTLE,
    )(place, asked, x)


def mirror_kernel(places_ref, counts_ref, first_ref, second_ref, own_ref, tiles_ref, tail_ref, out_ref, wide, sums):
    slots = tiles_ref.shape[0]
    part = first_ref.shape[0]
    wide[:part, :] = first_ref[...].astype(jnp.float32)
    wide[part : 2 * part, :] = second_ref[...].astype(jnp.float32)
    wide[2 * part : -8 * SHARE, :] = own_ref[...].astype(jnp.float32)
    wide[-8 * SHARE :, :] = jnp.zeros((8 * SHARE, LANES), jnp.float32)
    lanes = lax.broadcasted_iota(jnp.int32, (8, LANES), 1)
    for slot in range(slots):
        x = wide[pl.ds(places_ref[slot], 8, stride=SHARE), :]
        x = jnp.where(lanes < counts_ref[slot], x, 0.0).astype(jnp.bfloat16)
        y = lax.dot_general(x, tiles_ref[slot], (((1,), (0,)), ((), ())), preferred_element_type=jnp.float32)
        sums[pl.ds(slot, 8, stride=slots), :] = y
    out_ref[: 8 * slots, :] = sums[...].astype(jnp.bfloat16)
    out_ref[8 * slots :, :] = tail_ref[...]


def mirror_products(places, counts, first, second, own, tiles, tail):
    slots = tiles.shape[0]
    return pl.pallas_call(
        mirror_kernel,
        out_shape=jax.ShapeDtypeStruct((8 * slots + LIST_TAIL, LANES), jnp.bfloat16),
        in_specs=[SMEM, SMEM, VMEM, VMEM, VMEM, VMEM, VMEM],
        out_specs=VMEM,
        scratch_shapes=[
            pltpu.VMEM((2 * first.shape[0] + 3 * 8 * SHARE, LANES), jnp.float32),
            pltpu.VMEM((8 * slots, LANES), jnp.float32),
        ],
        compiler_params=PARAMS,
        cost_estimate=LITTLE,
    )(places, counts, first, second, own, tiles, tail)


def forward_kernel(places_ref, goals_ref, counts_ref, here_ref, there_ref, tiles_ref, first_ref, second_ref, own_ref, wide, sums):
    slots = tiles_ref.shape[0]
    half = here_ref.shape[0]
    part = first_ref.shape[0]
    wide[:half, :] = here_ref[...].astype(jnp.float32)
    wide[half:, :] = there_ref[...].astype(jnp.float32)
    sums[...] = jnp.zeros_like(sums)
    lanes = lax.broadcasted_iota(jnp.int32, (8, LANES), 1)
    for slot in range(slots):
        x = wide[pl.ds(pl.multiple_of(places_ref[slot] * 8, 8), 8), :].astype(jnp.bfloat16)
        y = lax.dot_general(x, tiles_ref[slot], (((1,), (1,)), ((), ())), preferred_element_type=jnp.float32)
        y = jnp.where(lanes < counts_ref[slot], y, 0.0)
        sums[pl.ds(goals_ref[slot], 8, stride=SHARE), :] = y
    first_ref[...] = sums[:part, :].astype(jnp.bfloat16)
    second_ref[...] = sums[part : 2 * part, :].astype(jnp.bfloat16)
    own_ref[...] = sums[2 * part : -8 * SHARE, :].astype(jnp.bfloat16)


def forward_products(places, goals, counts, here, there, tiles, cols):
    part = cols * 8 * SHARE
    shape = jax.ShapeDtypeStruct((part, LANES), jnp.bfloat16)
    own = jax.ShapeDtypeStruct((2 * 8 * SHARE, LANES), jnp.bfloat16)
    return pl.pallas_call(
        forward_kernel,
        out_shape=(shape, shape, own),
        in_specs=[SMEM, SMEM, SMEM, VMEM, VMEM, VMEM],
        out_specs=(VMEM, VMEM, VMEM),
        scratch_shapes=[
            pltpu.VMEM((2 * here.shape[0], LANES), jnp.float32),
            pltpu.VMEM((2 * part + 3 * 8 * SHARE, LANES), jnp.float32),
        ],
        compiler_params=PARAMS,
        cost_estimate=LITTLE,
    )(places, goals, counts, here, there, tiles)


def sum_kernel(cols, slots, place_ref, most_ref, asked_ref, first_ref, second_ref, own_ref, *refs):
    lists, (out_ref, acc) = refs[:-2], refs[-2:]
    tiles_here = out_ref.shape[0] // 8
    rows = 8 * slots + LIST_TAIL
    near = lax.broadcasted_iota(jnp.int32, (tiles_here, LANES), 0)
    own = (near + place_ref[2]).astype(jnp.float32)
    acc[...] = jnp.zeros_like(acc)

    def add_forward(ref, askers):
        chosen = [chosen_of(asked_ref, col, near)[:, start : start + SHARE] for col, start in askers]
        chosen = jnp.concatenate(chosen, axis=1).astype(jnp.bfloat16)
        for vec in range(8):
            values = [ref[(i * 8 + vec) * SHARE : (i * 8 + vec + 1) * SHARE, :] for i in range(len(askers))]
            acc[vec] += jnp.dot(chosen, jnp.concatenate(values, axis=0), preferred_element_type=jnp.float32)

    add_forward(first_ref, [(col, 0) for col in range(cols)])
    add_forward(own_ref, [(place_ref[0], 0), (place_ref[0], SHARE)])

    @pl.when(most_ref[0] > SHARE)
    def _():
        add_forward(second_ref, [(col, SHARE) for col in range(cols)])

    for part in lists:
        for start in range(0, part.shape[0], rows):
            digits = part[start + 8 * slots : start + rows, :].astype(jnp.float32)
            ids = digits[0:1] + 64.0 * digits[1:2] + 4096.0 * digits[2:3]
            chosen = jnp.where(own == ids, 1.0, 0.0)[:, :slots].astype(jnp.bfloat16)
            for vec in range(8):
                values = part[start + vec * slots : start + (vec + 1) * slots, :]
                acc[vec] += jnp.dot(chosen, values, preferred_element_type=jnp.float32)
    for vec in range(8):
        out_ref[pl.ds(vec, tiles_here, stride=8), :] = acc[vec]


def summed(place, most, asked, first, second, own, lists, slots, cols, tiles_here):
    return pl.pallas_call(
        functools.partial(sum_kernel, cols, slots),
        out_shape=jax.ShapeDtypeStruct((8 * tiles_here, LANES), jnp.float32),
        in_specs=[SMEM, SMEM] + [VMEM] * (4 + len(lists)),
        out_specs=VMEM,
        scratch_shapes=[pltpu.VMEM((8, tiles_here, LANES), jnp.float32)],
        compiler_params=PARAMS,
    )(place, most, asked, first, second, own, *lists)


def tail_of(ids):
    digits = jnp.stack([jnp.where(ids < 0, ids, ids % 64), jnp.maximum(ids, 0) // 64 % 64, jnp.maximum(ids, 0) // 4096])
    return jnp.pad(digits.astype(jnp.bfloat16), ((0, LIST_TAIL - 3), (0, LANES - ids.shape[0])))


def local(vectors, tiles, tile_rows, tile_cols, row_counts, live_tiles):
    vec_count, seg_len = vectors.shape
    slots, tile_len = tiles.shape[:2]
    rows, cols = lax.axis_size("row"), lax.axis_size("col")
    per_piece = seg_len // tile_len
    row, col = lax.axis_index("row"), lax.axis_index("col")
    grid = (rows, cols)
    join = functools.partial(jnp.concatenate, axis=0)

    live = jnp.arange(slots, dtype=jnp.int32) < live_tiles[0]
    counts = jnp.where(live, row_counts, 0)
    col_row = tile_cols // (cols * per_piece)
    group = col_row // 4 - row // 4
    other = (col_row % 4) ^ (row % 4)
    col_part = (other & 1) * 5 + jnp.where(group == 2, 4, (other >> 1) + 2 * group)
    col_places = col_part * per_piece + tile_cols % per_piece
    tail = tail_of(jnp.where(live, tile_cols, -1))

    rounded = vectors.astype(jnp.bfloat16).reshape(vec_count, per_piece, tile_len).transpose(1, 0, 2).reshape(-1, tile_len)
    place = jnp.stack([col, row * cols * per_piece, (row * cols + col) * per_piece])
    wanted, row_places = requests(place, tile_rows, live_tiles, cols, per_piece)
    across = across_halves(rounded, *grid)
    asked = lax.all_to_all(wanted, "col", 0, 0)
    most = jnp.max(asked[:, 1, 0])
    reply, late_reply, own_reply = replies(place, asked, rounded, cols, slots)
    both = join([rounded, after(across, reply)])
    groups = next_groups(both, *grid, -1)
    reply = over_columns(reply, cols)
    late_reply = lax.cond(most > SHARE, lambda v: over_columns(v, cols), lambda v: v, late_reply)
    here = join([both, *groups])
    there = other_core(here, *grid)
    mirror = mirror_products(row_places, counts, after(reply, here), late_reply, own_reply, tiles, tail)
    mirror_across = across_halves(mirror, *grid)
    there = after(there, mirror)
    forward, late_forward, own_forward = forward_products(col_places, row_places, counts, here, there, tiles, cols)
    mirror_both = join([mirror, after(mirror_across, forward)])
    mirror_groups = next_groups(mirror_both, *grid, 1)
    forward = over_columns(after(forward, mirror_both), cols)
    late_forward = lax.cond(most > SHARE, lambda v: over_columns(v, cols), lambda v: v, late_forward)
    mirror_here = after(join([mirror_both, *mirror_groups]), late_forward)
    mirror_there = other_core(mirror_here, *grid)
    lists = [mirror_here, mirror_there]
    total = summed(place, most.reshape(1), asked, forward, late_forward, own_forward, lists, slots, cols, per_piece)
    return total.reshape(per_piece, vec_count, tile_len).transpose(1, 0, 2).reshape(vec_count, seg_len)


def solution(mesh):
    placed = (
        P(None, AXES),
        P(AXES, None, None),
        P(AXES),
        P(AXES),
        P(AXES),
        P(AXES),
    )
    return jax.shard_map(local, mesh=mesh, in_specs=placed, out_specs=P(None, AXES), check_vma=False)
```

```python
import functools

import jax
import jax.numpy as jnp
from jax import lax
from jax.experimental import pallas as pl
from jax.experimental.pallas import tpu as pltpu
from jax.sharding import PartitionSpec as P

AXES = ("row", "col")
VMEM_BYTES = 40 * 1024 * 1024
LIST_TAIL = 16
SHARE = 32
LANES = 128
VMEM = pl.BlockSpec(memory_space=pltpu.VMEM)
SMEM = pl.BlockSpec(memory_space=pltpu.SMEM)
PARAMS = pltpu.CompilerParams(vmem_limit_bytes=VMEM_BYTES)
LITTLE = pl.CostEstimate(flops=0, bytes_accessed=0, transcendentals=0)


def send(value, moves):
    return lax.ppermute(value, AXES, moves)


def moves_of(rows, cols, target):
    pairs = []
    for row in range(rows):
        for col in range(cols):
            to = target(row, col)
            if to is not None and 0 <= to[0] < rows:
                pairs.append((row * cols + col, to[0] * cols + to[1]))
    return pairs


def across_halves(value, rows, cols):
    return send(value, moves_of(rows, cols, lambda r, c: (r ^ 2, c)))


def next_groups(both, rows, cols, way):
    last_half = 1 if way < 0 else 0
    count = both.shape[0] // 2
    return [
        send(both, moves_of(rows, cols, lambda r, c: (r + 4 * way, c))),
        send(
            both[count:],
            moves_of(rows, cols, lambda r, c: (r + 8 * way, c) if r // 2 % 2 == last_half else None),
        ),
    ]


def other_core(here, rows, cols):
    return send(here, moves_of(rows, cols, lambda r, c: (r ^ 1, c)))


def over_columns(value, cols):
    return lax.all_to_all(value.reshape(cols, -1, LANES), "col", 0, 0).reshape(-1, LANES)


def after(value, *others):
    return lax.optimization_barrier((value, *others))[0]


def request_kernel(cols, per_piece, place_ref, rows_ref, live_ref, ids_ref, places_ref, used, seen):
    slots = rows_ref.shape[0]
    me, start = place_ref[0], place_ref[1]
    for col in range(cols):
        used[col] = 0
    live = live_ref[0]
    for slot in range(slots):
        tile = rows_ref[slot] - start
        col = jnp.int32(0)
        for edge in range(1, cols):
            col = col + jnp.where(tile >= edge * per_piece, 1, 0)
        here = slot < live
        near = tile - col * per_piece
        count = used[col]
        known = jnp.minimum(seen[tile], slots - 1)
        again = (seen[tile] >= 0) & (seen[tile] < count) & (ids_ref[col, 0, jnp.maximum(known, 0)] == near)
        rank = jnp.where(again, known, count)
        used[col] = count + jnp.where(here & jnp.logical_not(again), 1, 0)
        ids_ref[col, 0, rank] = near
        seen[tile] = rank
        late = jnp.where(rank < SHARE, 0, 1)
        chunk = jnp.where(col == me, 2 * cols + late, col + cols * late)
        places_ref[slot] = jnp.where(here, chunk * (8 * SHARE) + rank - late * SHARE, (2 * cols + 2) * 8 * SHARE)
    most = jnp.int32(0)
    for col in range(cols):
        most = jnp.maximum(most, jnp.where(col == me, 0, used[col]))
    for col in range(cols):
        ids_ref[col, 1, 0] = most
        ids_ref[col, 1, 1] = used[col]


def requests(place, tile_rows, live_tiles, cols, per_piece):
    slots = tile_rows.shape[0]
    return pl.pallas_call(
        functools.partial(request_kernel, cols, per_piece),
        out_shape=(
            jax.ShapeDtypeStruct((cols, 8, LANES), jnp.int32),
            jax.ShapeDtypeStruct((slots,), jnp.int32),
        ),
        in_specs=[SMEM, SMEM, SMEM],
        out_specs=(SMEM, SMEM),
        scratch_shapes=[pltpu.SMEM((cols,), jnp.int32), pltpu.SMEM((cols * per_piece,), jnp.int32)],
        cost_estimate=LITTLE,
    )(place, tile_rows, live_tiles)


def chosen_of(asked_ref, col, places):
    lanes = lax.broadcasted_iota(jnp.int32, places.shape, 1)
    asked = (places == asked_ref[col, 0:1, :]) & (lanes < asked_ref[col, 1:2, 1:2])
    return jnp.where(asked, 1.0, 0.0)


def reply_kernel(cols, slots, place_ref, asked_ref, x_ref, first_ref, second_ref, own_ref, wide):
    tiles = x_ref.shape[0] // 8
    wide[...] = x_ref[...].astype(jnp.float32)
    places = lax.broadcasted_iota(jnp.int32, (LANES, LANES), 0)
    wanted = [chosen_of(asked_ref, col, places).T[:slots, :tiles] for col in [*range(cols), place_ref[0]]]
    wanted = jnp.concatenate(wanted, axis=0).astype(jnp.bfloat16)
    for vec in range(8):
        x = wide[pl.ds(vec, tiles, stride=8), :].astype(jnp.bfloat16)
        found = jnp.dot(wanted, x, preferred_element_type=jnp.float32).astype(jnp.bfloat16)
        for col in range(cols + 1):
            early = found[col * slots : col * slots + SHARE]
            late = found[col * slots + SHARE : (col + 1) * slots]
            at = (col * 8 + vec) * SHARE
            if col < cols:
                first_ref[at : at + SHARE, :] = early
                second_ref[at : at + SHARE, :] = late
            else:
                own_ref[vec * SHARE : (vec + 1) * SHARE, :] = early
                own_ref[(8 + vec) * SHARE : (9 + vec) * SHARE, :] = late


def replies(place, asked, x, cols, slots):
    shape = jax.ShapeDtypeStruct((cols * 8 * SHARE, LANES), jnp.bfloat16)
    own = jax.ShapeDtypeStruct((2 * 8 * SHARE, LANES), jnp.bfloat16)
    return pl.pallas_call(
        functools.partial(reply_kernel, cols, slots),
        out_shape=(shape, shape, own),
        in_specs=[SMEM, VMEM, VMEM],
        out_specs=(VMEM, VMEM, VMEM),
        scratch_shapes=[pltpu.VMEM(x.shape, jnp.float32)],
        compiler_params=PARAMS,
        cost_estimate=LITTLE,
    )(place, asked, x)


def mirror_kernel(places_ref, counts_ref, first_ref, second_ref, own_ref, tiles_ref, tail_ref, out_ref, wide, sums):
    slots = tiles_ref.shape[0]
    part = first_ref.shape[0]
    wide[:part, :] = first_ref[...].astype(jnp.float32)
    wide[part : 2 * part, :] = second_ref[...].astype(jnp.float32)
    wide[2 * part : -8 * SHARE, :] = own_ref[...].astype(jnp.float32)
    wide[-8 * SHARE :, :] = jnp.zeros((8 * SHARE, LANES), jnp.float32)
    lanes = lax.broadcasted_iota(jnp.int32, (8, LANES), 1)
    for slot in range(slots):
        x = wide[pl.ds(places_ref[slot], 8, stride=SHARE), :]
        x = jnp.where(lanes < counts_ref[slot], x, 0.0).astype(jnp.bfloat16)
        y = lax.dot_general(x, tiles_ref[slot], (((1,), (0,)), ((), ())), preferred_element_type=jnp.float32)
        sums[pl.ds(slot, 8, stride=slots), :] = y
    out_ref[: 8 * slots, :] = sums[...].astype(jnp.bfloat16)
    out_ref[8 * slots :, :] = tail_ref[...]


def mirror_products(places, counts, first, second, own, tiles, tail):
    slots = tiles.shape[0]
    return pl.pallas_call(
        mirror_kernel,
        out_shape=jax.ShapeDtypeStruct((8 * slots + LIST_TAIL, LANES), jnp.bfloat16),
        in_specs=[SMEM, SMEM, VMEM, VMEM, VMEM, VMEM, VMEM],
        out_specs=VMEM,
        scratch_shapes=[
            pltpu.VMEM((2 * first.shape[0] + 3 * 8 * SHARE, LANES), jnp.float32),
            pltpu.VMEM((8 * slots, LANES), jnp.float32),
        ],
        compiler_params=PARAMS,
        cost_estimate=LITTLE,
    )(places, counts, first, second, own, tiles, tail)


def forward_kernel(places_ref, goals_ref, counts_ref, here_ref, there_ref, tiles_ref, first_ref, second_ref, own_ref, wide, sums):
    slots = tiles_ref.shape[0]
    half = here_ref.shape[0]
    part = first_ref.shape[0]
    wide[:half, :] = here_ref[...].astype(jnp.float32)
    wide[half:, :] = there_ref[...].astype(jnp.float32)
    sums[...] = jnp.zeros_like(sums)
    lanes = lax.broadcasted_iota(jnp.int32, (8, LANES), 1)
    for slot in range(slots):
        x = wide[pl.ds(pl.multiple_of(places_ref[slot] * 8, 8), 8), :].astype(jnp.bfloat16)
        y = lax.dot_general(x, tiles_ref[slot], (((1,), (1,)), ((), ())), preferred_element_type=jnp.float32)
        y = jnp.where(lanes < counts_ref[slot], y, 0.0)
        sums[pl.ds(goals_ref[slot], 8, stride=SHARE), :] += y
    first_ref[...] = sums[:part, :].astype(jnp.bfloat16)
    second_ref[...] = sums[part : 2 * part, :].astype(jnp.bfloat16)
    own_ref[...] = sums[2 * part : -8 * SHARE, :].astype(jnp.bfloat16)


def forward_products(places, goals, counts, here, there, tiles, cols):
    part = cols * 8 * SHARE
    shape = jax.ShapeDtypeStruct((part, LANES), jnp.bfloat16)
    own = jax.ShapeDtypeStruct((2 * 8 * SHARE, LANES), jnp.bfloat16)
    return pl.pallas_call(
        forward_kernel,
        out_shape=(shape, shape, own),
        in_specs=[SMEM, SMEM, SMEM, VMEM, VMEM, VMEM],
        out_specs=(VMEM, VMEM, VMEM),
        scratch_shapes=[
            pltpu.VMEM((2 * here.shape[0], LANES), jnp.float32),
            pltpu.VMEM((2 * part + 3 * 8 * SHARE, LANES), jnp.float32),
        ],
        compiler_params=PARAMS,
        cost_estimate=LITTLE,
    )(places, goals, counts, here, there, tiles)


def sum_kernel(cols, slots, place_ref, most_ref, asked_ref, first_ref, second_ref, own_ref, *refs):
    lists, (out_ref, acc) = refs[:-2], refs[-2:]
    tiles_here = out_ref.shape[0] // 8
    rows = 8 * slots + LIST_TAIL
    near = lax.broadcasted_iota(jnp.int32, (tiles_here, LANES), 0)
    own = (near + place_ref[2]).astype(jnp.float32)
    acc[...] = jnp.zeros_like(acc)

    def add_forward(ref, askers):
        chosen = [chosen_of(asked_ref, col, near)[:, start : start + SHARE] for col, start in askers]
        chosen = jnp.concatenate(chosen, axis=1).astype(jnp.bfloat16)
        for vec in range(8):
            values = [ref[(i * 8 + vec) * SHARE : (i * 8 + vec + 1) * SHARE, :] for i in range(len(askers))]
            acc[vec] += jnp.dot(chosen, jnp.concatenate(values, axis=0), preferred_element_type=jnp.float32)

    add_forward(first_ref, [(col, 0) for col in range(cols)])
    add_forward(own_ref, [(place_ref[0], 0), (place_ref[0], SHARE)])

    @pl.when(most_ref[0] > SHARE)
    def _():
        add_forward(second_ref, [(col, SHARE) for col in range(cols)])

    for part in lists:
        for start in range(0, part.shape[0], rows):
            digits = part[start + 8 * slots : start + rows, :].astype(jnp.float32)
            ids = digits[0:1] + 64.0 * digits[1:2] + 4096.0 * digits[2:3]
            chosen = jnp.where(own == ids, 1.0, 0.0)[:, :slots].astype(jnp.bfloat16)
            for vec in range(8):
                values = part[start + vec * slots : start + (vec + 1) * slots, :]
                acc[vec] += jnp.dot(chosen, values, preferred_element_type=jnp.float32)
    for vec in range(8):
        out_ref[pl.ds(vec, tiles_here, stride=8), :] = acc[vec]


def summed(place, most, asked, first, second, own, lists, slots, cols, tiles_here):
    return pl.pallas_call(
        functools.partial(sum_kernel, cols, slots),
        out_shape=jax.ShapeDtypeStruct((8 * tiles_here, LANES), jnp.float32),
        in_specs=[SMEM, SMEM] + [VMEM] * (4 + len(lists)),
        out_specs=VMEM,
        scratch_shapes=[pltpu.VMEM((8, tiles_here, LANES), jnp.float32)],
        compiler_params=PARAMS,
    )(place, most, asked, first, second, own, *lists)


def tail_of(ids):
    digits = jnp.stack([jnp.where(ids < 0, ids, ids % 64), jnp.maximum(ids, 0) // 64 % 64, jnp.maximum(ids, 0) // 4096])
    return jnp.pad(digits.astype(jnp.bfloat16), ((0, LIST_TAIL - 3), (0, LANES - ids.shape[0])))


def local(vectors, tiles, tile_rows, tile_cols, row_counts, live_tiles):
    vec_count, seg_len = vectors.shape
    slots, tile_len = tiles.shape[:2]
    rows, cols = lax.axis_size("row"), lax.axis_size("col")
    per_piece = seg_len // tile_len
    row, col = lax.axis_index("row"), lax.axis_index("col")
    grid = (rows, cols)
    join = functools.partial(jnp.concatenate, axis=0)

    live = jnp.arange(slots, dtype=jnp.int32) < live_tiles[0]
    counts = jnp.where(live, row_counts, 0)
    col_row = tile_cols // (cols * per_piece)
    group = col_row // 4 - row // 4
    other = (col_row % 4) ^ (row % 4)
    col_part = (other & 1) * 5 + jnp.where(group == 2, 4, (other >> 1) + 2 * group)
    col_places = col_part * per_piece + tile_cols % per_piece
    tail = tail_of(jnp.where(live, tile_cols, -1))

    rounded = vectors.astype(jnp.bfloat16).reshape(vec_count, per_piece, tile_len).transpose(1, 0, 2).reshape(-1, tile_len)
    place = jnp.stack([col, row * cols * per_piece, (row * cols + col) * per_piece])
    wanted, row_places = requests(place, tile_rows, live_tiles, cols, per_piece)
    across = across_halves(rounded, *grid)
    asked = lax.all_to_all(wanted, "col", 0, 0)
    most = jnp.max(asked[:, 1, 0])
    reply, late_reply, own_reply = replies(place, asked, rounded, cols, slots)
    both = join([rounded, after(across, reply)])
    groups = next_groups(both, *grid, -1)
    reply = over_columns(reply, cols)
    late_reply = lax.cond(most > SHARE, lambda v: over_columns(v, cols), lambda v: v, late_reply)
    here = join([both, *groups])
    there = other_core(here, *grid)
    mirror = mirror_products(row_places, counts, after(reply, here), late_reply, own_reply, tiles, tail)
    mirror_across = across_halves(mirror, *grid)
    there = after(there, mirror)
    forward, late_forward, own_forward = forward_products(col_places, row_places, counts, here, there, tiles, cols)
    mirror_both = join([mirror, after(mirror_across, forward)])
    mirror_groups = next_groups(mirror_both, *grid, 1)
    forward = over_columns(after(forward, mirror_both), cols)
    late_forward = lax.cond(most > SHARE, lambda v: over_columns(v, cols), lambda v: v, late_forward)
    mirror_here = after(join([mirror_both, *mirror_groups]), late_forward)
    mirror_there = other_core(mirror_here, *grid)
    lists = [mirror_here, mirror_there]
    total = summed(place, most.reshape(1), asked, forward, late_forward, own_forward, lists, slots, cols, per_piece)
    return total.reshape(per_piece, vec_count, tile_len).transpose(1, 0, 2).reshape(vec_count, seg_len)


def solution(mesh):
    placed = (
        P(None, AXES),
        P(AXES, None, None),
        P(AXES),
        P(AXES),
        P(AXES),
        P(AXES),
    )
    return jax.shard_map(local, mesh=mesh, in_specs=placed, out_specs=P(None, AXES), check_vma=False)
```

```python
import functools

import jax
import jax.numpy as jnp
from jax import lax
from jax.experimental import pallas as pl
from jax.experimental.pallas import tpu as pltpu
from jax.sharding import PartitionSpec as P

AXES = ("row", "col")
VMEM_BYTES = 40 * 1024 * 1024
LIST_TAIL = 16
SHARE = 32
LANES = 128
VMEM = pl.BlockSpec(memory_space=pltpu.VMEM)
SMEM = pl.BlockSpec(memory_space=pltpu.SMEM)
PARAMS = pltpu.CompilerParams(vmem_limit_bytes=VMEM_BYTES)
LITTLE = pl.CostEstimate(flops=0, bytes_accessed=0, transcendentals=0)


def send(value, moves):
    return lax.ppermute(value, AXES, moves)


def moves_of(rows, cols, target):
    pairs = []
    for row in range(rows):
        for col in range(cols):
            to = target(row, col)
            if to is not None and 0 <= to[0] < rows:
                pairs.append((row * cols + col, to[0] * cols + to[1]))
    return pairs


def across_halves(value, rows, cols):
    return send(value, moves_of(rows, cols, lambda r, c: (r ^ 2, c)))


def next_groups(both, rows, cols, way):
    last_half = 1 if way < 0 else 0
    count = both.shape[0] // 2
    return [
        send(both, moves_of(rows, cols, lambda r, c: (r + 4 * way, c))),
        send(
            both[count:],
            moves_of(rows, cols, lambda r, c: (r + 8 * way, c) if r // 2 % 2 == last_half else None),
        ),
    ]


def other_core(here, rows, cols):
    return send(here, moves_of(rows, cols, lambda r, c: (r ^ 1, c)))


def over_columns(value, cols):
    return lax.all_to_all(value.reshape(cols, -1, LANES), "col", 0, 0).reshape(-1, LANES)


def after(value, *others):
    return lax.optimization_barrier((value, *others))[0]


def request_kernel(cols, per_piece, place_ref, rows_ref, live_ref, ids_ref, places_ref, used, seen):
    slots = rows_ref.shape[0]
    me, start = place_ref[0], place_ref[1]
    for col in range(cols):
        used[col] = 0
    live = live_ref[0]
    for slot in range(slots):
        tile = rows_ref[slot] - start
        col = jnp.int32(0)
        for edge in range(1, cols):
            col = col + jnp.where(tile >= edge * per_piece, 1, 0)
        here = slot < live
        near = tile - col * per_piece
        count = used[col]
        known = jnp.minimum(seen[tile], slots - 1)
        again = (seen[tile] >= 0) & (seen[tile] < count) & (ids_ref[col, 0, jnp.maximum(known, 0)] == near)
        rank = jnp.where(again, known, count)
        used[col] = count + jnp.where(here & jnp.logical_not(again), 1, 0)
        ids_ref[col, 0, rank] = near
        seen[tile] = rank
        late = jnp.where(rank < SHARE, 0, 1)
        chunk = jnp.where(col == me, 2 * cols + late, col + cols * late)
        places_ref[slot] = jnp.where(here, chunk * (8 * SHARE) + rank - late * SHARE, (2 * cols + 2) * 8 * SHARE)
    most = jnp.int32(0)
    for col in range(cols):
        most = jnp.maximum(most, jnp.where(col == me, 0, used[col]))
    for col in range(cols):
        ids_ref[col, 1, 0] = most
        ids_ref[col, 1, 1] = used[col]


def requests(place, tile_rows, live_tiles, cols, per_piece):
    slots = tile_rows.shape[0]
    return pl.pallas_call(
        functools.partial(request_kernel, cols, per_piece),
        out_shape=(
            jax.ShapeDtypeStruct((cols, 8, LANES), jnp.int32),
            jax.ShapeDtypeStruct((slots,), jnp.int32),
        ),
        in_specs=[SMEM, SMEM, SMEM],
        out_specs=(SMEM, SMEM),
        scratch_shapes=[pltpu.SMEM((cols,), jnp.int32), pltpu.SMEM((cols * per_piece,), jnp.int32)],
        cost_estimate=LITTLE,
    )(place, tile_rows, live_tiles)


def chosen_of(asked_ref, col, places):
    lanes = lax.broadcasted_iota(jnp.int32, places.shape, 1)
    asked = (places == asked_ref[col, 0:1, :]) & (lanes < asked_ref[col, 1:2, 1:2])
    return jnp.where(asked, 1.0, 0.0)


def reply_kernel(cols, slots, place_ref, asked_ref, x_ref, first_ref, second_ref, own_ref, wide):
    tiles = x_ref.shape[0] // 8
    wide[...] = x_ref[...].astype(jnp.float32)
    places = lax.broadcasted_iota(jnp.int32, (LANES, LANES), 0)
    wanted = [chosen_of(asked_ref, col, places).T[:slots, :tiles] for col in [*range(cols), place_ref[0]]]
    wanted = jnp.concatenate(wanted, axis=0).astype(jnp.bfloat16)
    for vec in range(8):
        x = wide[pl.ds(vec, tiles, stride=8), :].astype(jnp.bfloat16)
        found = jnp.dot(wanted, x, preferred_element_type=jnp.float32).astype(jnp.bfloat16)
        for col in range(cols + 1):
            early = found[col * slots : col * slots + SHARE]
            late = found[col * slots + SHARE : (col + 1) * slots]
            at = (col * 8 + vec) * SHARE
            if col < cols:
                first_ref[at : at + SHARE, :] = early
                second_ref[at : at + SHARE, :] = late
            else:
                own_ref[vec * SHARE : (vec + 1) * SHARE, :] = early
                own_ref[(8 + vec) * SHARE : (9 + vec) * SHARE, :] = late


def replies(place, asked, x, cols, slots):
    shape = jax.ShapeDtypeStruct((cols * 8 * SHARE, LANES), jnp.bfloat16)
    own = jax.ShapeDtypeStruct((2 * 8 * SHARE, LANES), jnp.bfloat16)
    return pl.pallas_call(
        functools.partial(reply_kernel, cols, slots),
        out_shape=(shape, shape, own),
        in_specs=[SMEM, VMEM, VMEM],
        out_specs=(VMEM, VMEM, VMEM),
        scratch_shapes=[pltpu.VMEM(x.shape, jnp.float32)],
        compiler_params=PARAMS,
        cost_estimate=LITTLE,
    )(place, asked, x)


def mirror_kernel(places_ref, counts_ref, first_ref, second_ref, own_ref, tiles_ref, tail_ref, out_ref, wide, sums):
    slots = tiles_ref.shape[0]
    part = first_ref.shape[0]
    wide[:part, :] = first_ref[...].astype(jnp.float32)
    wide[part : 2 * part, :] = second_ref[...].astype(jnp.float32)
    wide[2 * part : -8 * SHARE, :] = own_ref[...].astype(jnp.float32)
    wide[-8 * SHARE :, :] = jnp.zeros((8 * SHARE, LANES), jnp.float32)
    lanes = lax.broadcasted_iota(jnp.int32, (8, LANES), 1)
    for slot in range(slots):
        x = wide[pl.ds(places_ref[slot], 8, stride=SHARE), :]
        x = jnp.where(lanes < counts_ref[slot], x, 0.0).astype(jnp.bfloat16)
        y = lax.dot_general(x, tiles_ref[slot], (((1,), (0,)), ((), ())), preferred_element_type=jnp.float32)
        sums[pl.ds(slot, 8, stride=slots), :] = y
    out_ref[: 8 * slots, :] = sums[...].astype(jnp.bfloat16)
    out_ref[8 * slots :, :] = tail_ref[...]


def mirror_products(places, counts, first, second, own, tiles, tail):
    slots = tiles.shape[0]
    return pl.pallas_call(
        mirror_kernel,
        out_shape=jax.ShapeDtypeStruct((8 * slots + LIST_TAIL, LANES), jnp.bfloat16),
        in_specs=[SMEM, SMEM, VMEM, VMEM, VMEM, VMEM, VMEM],
        out_specs=VMEM,
        scratch_shapes=[
            pltpu.VMEM((2 * first.shape[0] + 3 * 8 * SHARE, LANES), jnp.float32),
            pltpu.VMEM((8 * slots, LANES), jnp.float32),
        ],
        compiler_params=PARAMS,
        cost_estimate=LITTLE,
    )(places, counts, first, second, own, tiles, tail)


def forward_kernel(places_ref, goals_ref, counts_ref, here_ref, there_ref, tiles_ref, first_ref, second_ref, own_ref, wide, sums):
    slots = tiles_ref.shape[0]
    half = here_ref.shape[0]
    part = first_ref.shape[0]
    wide[:half, :] = here_ref[...].astype(jnp.float32)
    wide[half:, :] = there_ref[...].astype(jnp.float32)
    sums[...] = jnp.zeros_like(sums)
    lanes = lax.broadcasted_iota(jnp.int32, (8, LANES), 1)
    for slot in range(slots):
        x = wide[pl.ds(pl.multiple_of(places_ref[slot] * 8, 8), 8), :].astype(jnp.bfloat16)
        y = lax.dot_general(x, tiles_ref[slot], (((1,), (1,)), ((), ())), preferred_element_type=jnp.float32)
        y = jnp.where(lanes < counts_ref[slot], y, 0.0)
        sums[pl.ds(goals_ref[slot], 8, stride=SHARE), :] += y
    first_ref[...] = sums[:part, :].astype(jnp.bfloat16)
    second_ref[...] = sums[part : 2 * part, :].astype(jnp.bfloat16)
    own_ref[...] = sums[2 * part : -8 * SHARE, :].astype(jnp.bfloat16)


def forward_products(places, goals, counts, here, there, tiles, cols):
    part = cols * 8 * SHARE
    shape = jax.ShapeDtypeStruct((part, LANES), jnp.bfloat16)
    own = jax.ShapeDtypeStruct((2 * 8 * SHARE, LANES), jnp.bfloat16)
    return pl.pallas_call(
        forward_kernel,
        out_shape=(shape, shape, own),
        in_specs=[SMEM, SMEM, SMEM, VMEM, VMEM, VMEM],
        out_specs=(VMEM, VMEM, VMEM),
        scratch_shapes=[
            pltpu.VMEM((2 * here.shape[0], LANES), jnp.float32),
            pltpu.VMEM((2 * part + 3 * 8 * SHARE, LANES), jnp.float32),
        ],
        compiler_params=PARAMS,
        cost_estimate=LITTLE,
    )(places, goals, counts, here, there, tiles)


def add_lists(lists, own, slots, acc):
    rows = 8 * slots + LIST_TAIL
    for part in lists:
        for start in range(0, part.shape[0], rows):
            digits = part[start + 8 * slots : start + rows, :].astype(jnp.float32)
            ids = digits[0:1] + 64.0 * digits[1:2] + 4096.0 * digits[2:3]
            chosen = jnp.where(own == ids, 1.0, 0.0)[:, :slots].astype(jnp.bfloat16)
            for vec in range(8):
                values = part[start + vec * slots : start + (vec + 1) * slots, :]
                acc[vec] += jnp.dot(chosen, values, preferred_element_type=jnp.float32)


def own_tiles(place_ref, tiles_here):
    return (lax.broadcasted_iota(jnp.int32, (tiles_here, LANES), 0) + place_ref[2]).astype(jnp.float32)


def first_sum_kernel(cols, slots, place_ref, most_ref, asked_ref, first_ref, second_ref, own_ref, list_ref, acc):
    tiles_here = acc.shape[1]
    near = lax.broadcasted_iota(jnp.int32, (tiles_here, LANES), 0)
    acc[...] = jnp.zeros_like(acc)

    def add_forward(ref, askers):
        chosen = [chosen_of(asked_ref, col, near)[:, start : start + SHARE] for col, start in askers]
        chosen = jnp.concatenate(chosen, axis=1).astype(jnp.bfloat16)
        for vec in range(8):
            values = [ref[(i * 8 + vec) * SHARE : (i * 8 + vec + 1) * SHARE, :] for i in range(len(askers))]
            acc[vec] += jnp.dot(chosen, jnp.concatenate(values, axis=0), preferred_element_type=jnp.float32)

    add_forward(first_ref, [(col, 0) for col in range(cols)])
    add_forward(own_ref, [(place_ref[0], 0), (place_ref[0], SHARE)])

    @pl.when(most_ref[0] > SHARE)
    def _():
        add_forward(second_ref, [(col, SHARE) for col in range(cols)])

    add_lists([list_ref], own_tiles(place_ref, tiles_here), slots, acc)


def first_sum(place, most, asked, first, second, own, some, slots, cols, tiles_here):
    return pl.pallas_call(
        functools.partial(first_sum_kernel, cols, slots),
        out_shape=jax.ShapeDtypeStruct((8, tiles_here, LANES), jnp.float32),
        in_specs=[SMEM, SMEM] + [VMEM] * 5,
        out_specs=VMEM,
        compiler_params=PARAMS,
        cost_estimate=LITTLE,
    )(place, most, asked, first, second, own, some)


def last_sum_kernel(slots, place_ref, start_ref, list_ref, out_ref, acc):
    tiles_here = acc.shape[1]
    acc[...] = start_ref[...]
    add_lists([list_ref], own_tiles(place_ref, tiles_here), slots, acc)
    for vec in range(8):
        out_ref[pl.ds(vec, tiles_here, stride=8), :] = acc[vec]


def last_sum(place, start, some, slots):
    tiles_here = start.shape[1]
    return pl.pallas_call(
        functools.partial(last_sum_kernel, slots),
        out_shape=jax.ShapeDtypeStruct((8 * tiles_here, LANES), jnp.float32),
        in_specs=[SMEM, VMEM, VMEM],
        out_specs=VMEM,
        scratch_shapes=[pltpu.VMEM(start.shape, jnp.float32)],
        compiler_params=PARAMS,
        cost_estimate=LITTLE,
    )(place, start, some)


def tail_of(ids):
    digits = jnp.stack([jnp.where(ids < 0, ids, ids % 64), jnp.maximum(ids, 0) // 64 % 64, jnp.maximum(ids, 0) // 4096])
    return jnp.pad(digits.astype(jnp.bfloat16), ((0, LIST_TAIL - 3), (0, LANES - ids.shape[0])))


def local(vectors, tiles, tile_rows, tile_cols, row_counts, live_tiles):
    vec_count, seg_len = vectors.shape
    slots, tile_len = tiles.shape[:2]
    rows, cols = lax.axis_size("row"), lax.axis_size("col")
    per_piece = seg_len // tile_len
    row, col = lax.axis_index("row"), lax.axis_index("col")
    grid = (rows, cols)
    join = functools.partial(jnp.concatenate, axis=0)

    live = jnp.arange(slots, dtype=jnp.int32) < live_tiles[0]
    counts = jnp.where(live, row_counts, 0)
    col_row = tile_cols // (cols * per_piece)
    group = col_row // 4 - row // 4
    other = (col_row % 4) ^ (row % 4)
    col_part = (other & 1) * 5 + jnp.where(group == 2, 4, (other >> 1) + 2 * group)
    col_places = col_part * per_piece + tile_cols % per_piece
    tail = tail_of(jnp.where(live, tile_cols, -1))

    rounded = vectors.astype(jnp.bfloat16).reshape(vec_count, per_piece, tile_len).transpose(1, 0, 2).reshape(-1, tile_len)
    place = jnp.stack([col, row * cols * per_piece, (row * cols + col) * per_piece])
    wanted, row_places = requests(place, tile_rows, live_tiles, cols, per_piece)
    across = across_halves(rounded, *grid)
    asked = lax.all_to_all(wanted, "col", 0, 0)
    most = jnp.max(asked[:, 1, 0])
    reply, late_reply, own_reply = replies(place, asked, rounded, cols, slots)
    both = join([rounded, after(across, reply)])
    groups = next_groups(both, *grid, -1)
    reply = over_columns(reply, cols)
    late_reply = lax.cond(most > SHARE, lambda v: over_columns(v, cols), lambda v: v, late_reply)
    here = join([both, *groups])
    there = other_core(here, *grid)
    mirror = mirror_products(row_places, counts, after(reply, here), late_reply, own_reply, tiles, tail)
    mirror_across = across_halves(mirror, *grid)
    there = after(there, mirror)
    forward, late_forward, own_forward = forward_products(col_places, row_places, counts, here, there, tiles, cols)
    mirror_both = join([mirror, after(mirror_across, forward)])
    mirror_groups = next_groups(mirror_both, *grid, 1)
    forward = over_columns(forward, cols)
    late_forward = lax.cond(most > SHARE, lambda v: over_columns(v, cols), lambda v: v, late_forward)
    mirror_here = after(join([mirror_both, *mirror_groups]), late_forward, forward)
    mirror_there = other_core(mirror_here, *grid)
    partial = first_sum(
        place, most.reshape(1), asked, forward, late_forward, own_forward, mirror_here, slots, cols, per_piece
    )
    total = last_sum(place, partial, mirror_there, slots)
    return total.reshape(per_piece, vec_count, tile_len).transpose(1, 0, 2).reshape(vec_count, seg_len)


def solution(mesh):
    placed = (
        P(None, AXES),
        P(AXES, None, None),
        P(AXES),
        P(AXES),
        P(AXES),
        P(AXES),
    )
    return jax.shard_map(local, mesh=mesh, in_specs=placed, out_specs=P(None, AXES), check_vma=False)
```

```python
import functools

import jax
import jax.numpy as jnp
from jax import lax
from jax.experimental import pallas as pl
from jax.experimental.pallas import tpu as pltpu
from jax.sharding import PartitionSpec as P

AXES = ("row", "col")
VMEM_BYTES = 40 * 1024 * 1024
LIST_TAIL = 16
SHARE = 32
LANES = 128
VMEM = pl.BlockSpec(memory_space=pltpu.VMEM)
SMEM = pl.BlockSpec(memory_space=pltpu.SMEM)
PARAMS = pltpu.CompilerParams(vmem_limit_bytes=VMEM_BYTES)
LITTLE = pl.CostEstimate(flops=0, bytes_accessed=0, transcendentals=0)


def send(value, moves):
    return lax.ppermute(value, AXES, moves)


def moves_of(rows, cols, target):
    pairs = []
    for row in range(rows):
        for col in range(cols):
            to = target(row, col)
            if to is not None and 0 <= to[0] < rows:
                pairs.append((row * cols + col, to[0] * cols + to[1]))
    return pairs


def across_halves(value, rows, cols):
    return send(value, moves_of(rows, cols, lambda r, c: (r ^ 2, c)))


def next_groups(both, rows, cols, way):
    last_half = 1 if way < 0 else 0
    count = both.shape[0] // 2
    return [
        send(both, moves_of(rows, cols, lambda r, c: (r + 4 * way, c))),
        send(
            both[count:],
            moves_of(rows, cols, lambda r, c: (r + 8 * way, c) if r // 2 % 2 == last_half else None),
        ),
    ]


def other_core(here, rows, cols):
    return send(here, moves_of(rows, cols, lambda r, c: (r ^ 1, c)))


def over_columns(value, cols):
    return lax.all_to_all(value.reshape(cols, -1, LANES), "col", 0, 0).reshape(-1, LANES)


def after(value, *others):
    return lax.optimization_barrier((value, *others))[0]


def request_kernel(cols, per_piece, place_ref, rows_ref, live_ref, ids_ref, places_ref, used, seen):
    slots = rows_ref.shape[0]
    me, start = place_ref[0], place_ref[1]
    for col in range(cols):
        used[col] = 0
    live = live_ref[0]
    for slot in range(slots):
        tile = rows_ref[slot] - start
        col = jnp.int32(0)
        for edge in range(1, cols):
            col = col + jnp.where(tile >= edge * per_piece, 1, 0)
        here = slot < live
        near = tile - col * per_piece
        count = used[col]
        known = jnp.minimum(seen[tile], slots - 1)
        again = (seen[tile] >= 0) & (seen[tile] < count) & (ids_ref[col, 0, jnp.maximum(known, 0)] == near)
        rank = jnp.where(again, known, count)
        used[col] = count + jnp.where(here & jnp.logical_not(again), 1, 0)
        ids_ref[col, 0, rank] = near
        seen[tile] = rank
        late = jnp.where(rank < SHARE, 0, 1)
        chunk = jnp.where(col == me, 2 * cols + late, col + cols * late)
        places_ref[slot] = jnp.where(here, chunk * (8 * SHARE) + rank - late * SHARE, (2 * cols + 2) * 8 * SHARE)
    most = jnp.int32(0)
    for col in range(cols):
        most = jnp.maximum(most, jnp.where(col == me, 0, used[col]))
    for col in range(cols):
        ids_ref[col, 1, 0] = most
        ids_ref[col, 1, 1] = used[col]


def requests(place, tile_rows, live_tiles, cols, per_piece):
    slots = tile_rows.shape[0]
    return pl.pallas_call(
        functools.partial(request_kernel, cols, per_piece),
        out_shape=(
            jax.ShapeDtypeStruct((cols, 8, LANES), jnp.int32),
            jax.ShapeDtypeStruct((slots,), jnp.int32),
        ),
        in_specs=[SMEM, SMEM, SMEM],
        out_specs=(SMEM, SMEM),
        scratch_shapes=[pltpu.SMEM((cols,), jnp.int32), pltpu.SMEM((cols * per_piece,), jnp.int32)],
        cost_estimate=LITTLE,
    )(place, tile_rows, live_tiles)


def chosen_of(asked_ref, col, places):
    lanes = lax.broadcasted_iota(jnp.int32, places.shape, 1)
    asked = (places == asked_ref[col, 0:1, :]) & (lanes < asked_ref[col, 1:2, 1:2])
    return jnp.where(asked, 1.0, 0.0)


def reply_kernel(cols, slots, place_ref, asked_ref, x_ref, first_ref, second_ref, own_ref, wide):
    tiles = x_ref.shape[0] // 8
    wide[...] = x_ref[...].astype(jnp.float32)
    places = lax.broadcasted_iota(jnp.int32, (LANES, LANES), 0)
    wanted = [chosen_of(asked_ref, col, places).T[:slots, :tiles] for col in [*range(cols), place_ref[0]]]
    wanted = jnp.concatenate(wanted, axis=0).astype(jnp.bfloat16)
    for vec in range(8):
        x = wide[pl.ds(vec, tiles, stride=8), :].astype(jnp.bfloat16)
        found = jnp.dot(wanted, x, preferred_element_type=jnp.float32).astype(jnp.bfloat16)
        for col in range(cols + 1):
            early = found[col * slots : col * slots + SHARE]
            late = found[col * slots + SHARE : (col + 1) * slots]
            at = (col * 8 + vec) * SHARE
            if col < cols:
                first_ref[at : at + SHARE, :] = early
                second_ref[at : at + SHARE, :] = late
            else:
                own_ref[vec * SHARE : (vec + 1) * SHARE, :] = early
                own_ref[(8 + vec) * SHARE : (9 + vec) * SHARE, :] = late


def replies(place, asked, x, cols, slots):
    shape = jax.ShapeDtypeStruct((cols * 8 * SHARE, LANES), jnp.bfloat16)
    own = jax.ShapeDtypeStruct((2 * 8 * SHARE, LANES), jnp.bfloat16)
    return pl.pallas_call(
        functools.partial(reply_kernel, cols, slots),
        out_shape=(shape, shape, own),
        in_specs=[SMEM, VMEM, VMEM],
        out_specs=(VMEM, VMEM, VMEM),
        scratch_shapes=[pltpu.VMEM(x.shape, jnp.float32)],
        compiler_params=PARAMS,
        cost_estimate=LITTLE,
    )(place, asked, x)


def mirror_kernel(places_ref, counts_ref, first_ref, second_ref, own_ref, tiles_ref, tail_ref, out_ref, wide, sums):
    slots = tiles_ref.shape[0]
    part = first_ref.shape[0]
    wide[:part, :] = first_ref[...].astype(jnp.float32)
    wide[part : 2 * part, :] = second_ref[...].astype(jnp.float32)
    wide[2 * part : -8 * SHARE, :] = own_ref[...].astype(jnp.float32)
    wide[-8 * SHARE :, :] = jnp.zeros((8 * SHARE, LANES), jnp.float32)
    lanes = lax.broadcasted_iota(jnp.int32, (8, LANES), 1)
    for slot in range(slots):
        x = wide[pl.ds(places_ref[slot], 8, stride=SHARE), :]
        x = jnp.where(lanes < counts_ref[slot], x, 0.0).astype(jnp.bfloat16)
        y = lax.dot_general(x, tiles_ref[slot], (((1,), (0,)), ((), ())), preferred_element_type=jnp.float32)
        sums[pl.ds(slot, 8, stride=slots), :] = y
    out_ref[: 8 * slots, :] = sums[...].astype(jnp.bfloat16)
    out_ref[8 * slots :, :] = tail_ref[...]


def mirror_products(places, counts, first, second, own, tiles, tail):
    slots = tiles.shape[0]
    return pl.pallas_call(
        mirror_kernel,
        out_shape=jax.ShapeDtypeStruct((8 * slots + LIST_TAIL, LANES), jnp.bfloat16),
        in_specs=[SMEM, SMEM, VMEM, VMEM, VMEM, VMEM, VMEM],
        out_specs=VMEM,
        scratch_shapes=[
            pltpu.VMEM((2 * first.shape[0] + 3 * 8 * SHARE, LANES), jnp.float32),
            pltpu.VMEM((8 * slots, LANES), jnp.float32),
        ],
        compiler_params=PARAMS,
        cost_estimate=LITTLE,
    )(places, counts, first, second, own, tiles, tail)


def forward_kernel(places_ref, goals_ref, counts_ref, here_ref, there_ref, tiles_ref, first_ref, second_ref, own_ref, sums):
    slots = tiles_ref.shape[0]
    half = here_ref.shape[0] // 8
    part = first_ref.shape[0]
    sums[...] = jnp.zeros_like(sums)
    lanes = lax.broadcasted_iota(jnp.int32, (8, LANES), 1)
    for slot in range(slots):
        place = places_ref[slot]
        near = place < half
        place = jnp.where(near, place, place - half)
        rows = pl.ds(pl.multiple_of(lax.shift_right_logical(place, 1) * 16, 16), 16)
        pair = jnp.where(near, here_ref[rows, :].astype(jnp.float32), there_ref[rows, :].astype(jnp.float32))
        x = jnp.where((place & 1) == 0, pair[:8], pair[8:]).astype(jnp.bfloat16)
        y = lax.dot_general(x, tiles_ref[slot], (((1,), (1,)), ((), ())), preferred_element_type=jnp.float32)
        y = jnp.where(lanes < counts_ref[slot], y, 0.0)
        sums[pl.ds(goals_ref[slot], 8, stride=SHARE), :] += y
    first_ref[...] = sums[:part, :].astype(jnp.bfloat16)
    second_ref[...] = sums[part : 2 * part, :].astype(jnp.bfloat16)
    own_ref[...] = sums[2 * part : -8 * SHARE, :].astype(jnp.bfloat16)


def forward_products(places, goals, counts, here, there, tiles, cols):
    part = cols * 8 * SHARE
    shape = jax.ShapeDtypeStruct((part, LANES), jnp.bfloat16)
    own = jax.ShapeDtypeStruct((2 * 8 * SHARE, LANES), jnp.bfloat16)
    return pl.pallas_call(
        forward_kernel,
        out_shape=(shape, shape, own),
        in_specs=[SMEM, SMEM, SMEM, VMEM, VMEM, VMEM],
        out_specs=(VMEM, VMEM, VMEM),
        scratch_shapes=[
            pltpu.VMEM((2 * part + 3 * 8 * SHARE, LANES), jnp.float32),
        ],
        compiler_params=PARAMS,
        cost_estimate=LITTLE,
    )(places, goals, counts, here, there, tiles)


def add_lists(lists, own, slots, acc):
    rows = 8 * slots + LIST_TAIL
    for part in lists:
        for start in range(0, part.shape[0], rows):
            digits = part[start + 8 * slots : start + rows, :].astype(jnp.float32)
            ids = digits[0:1] + 64.0 * digits[1:2] + 4096.0 * digits[2:3]
            chosen = jnp.where(own == ids, 1.0, 0.0)[:, :slots].astype(jnp.bfloat16)
            for vec in range(8):
                values = part[start + vec * slots : start + (vec + 1) * slots, :]
                acc[vec] += jnp.dot(chosen, values, preferred_element_type=jnp.float32)


def own_tiles(place_ref, tiles_here):
    return (lax.broadcasted_iota(jnp.int32, (tiles_here, LANES), 0) + place_ref[2]).astype(jnp.float32)


def first_sum_kernel(cols, slots, place_ref, most_ref, asked_ref, first_ref, second_ref, own_ref, list_ref, acc):
    tiles_here = acc.shape[1]
    near = lax.broadcasted_iota(jnp.int32, (tiles_here, LANES), 0)
    acc[...] = jnp.zeros_like(acc)

    def add_forward(ref, askers):
        chosen = [chosen_of(asked_ref, col, near)[:, start : start + SHARE] for col, start in askers]
        chosen = jnp.concatenate(chosen, axis=1).astype(jnp.bfloat16)
        for vec in range(8):
            values = [ref[(i * 8 + vec) * SHARE : (i * 8 + vec + 1) * SHARE, :] for i in range(len(askers))]
            acc[vec] += jnp.dot(chosen, jnp.concatenate(values, axis=0), preferred_element_type=jnp.float32)

    add_forward(first_ref, [(col, 0) for col in range(cols)])
    add_forward(own_ref, [(place_ref[0], 0), (place_ref[0], SHARE)])

    @pl.when(most_ref[0] > SHARE)
    def _():
        add_forward(second_ref, [(col, SHARE) for col in range(cols)])

    add_lists([list_ref], own_tiles(place_ref, tiles_here), slots, acc)


def first_sum(place, most, asked, first, second, own, some, slots, cols, tiles_here):
    return pl.pallas_call(
        functools.partial(first_sum_kernel, cols, slots),
        out_shape=jax.ShapeDtypeStruct((8, tiles_here, LANES), jnp.float32),
        in_specs=[SMEM, SMEM] + [VMEM] * 5,
        out_specs=VMEM,
        compiler_params=PARAMS,
        cost_estimate=LITTLE,
    )(place, most, asked, first, second, own, some)


def last_sum_kernel(slots, place_ref, start_ref, list_ref, out_ref, acc):
    tiles_here = acc.shape[1]
    acc[...] = start_ref[...]
    add_lists([list_ref], own_tiles(place_ref, tiles_here), slots, acc)
    for vec in range(8):
        out_ref[pl.ds(vec, tiles_here, stride=8), :] = acc[vec]


def last_sum(place, start, some, slots):
    tiles_here = start.shape[1]
    return pl.pallas_call(
        functools.partial(last_sum_kernel, slots),
        out_shape=jax.ShapeDtypeStruct((8 * tiles_here, LANES), jnp.float32),
        in_specs=[SMEM, VMEM, VMEM],
        out_specs=VMEM,
        scratch_shapes=[pltpu.VMEM(start.shape, jnp.float32)],
        compiler_params=PARAMS,
        cost_estimate=LITTLE,
    )(place, start, some)


def tail_of(ids):
    digits = jnp.stack([jnp.where(ids < 0, ids, ids % 64), jnp.maximum(ids, 0) // 64 % 64, jnp.maximum(ids, 0) // 4096])
    return jnp.pad(digits.astype(jnp.bfloat16), ((0, LIST_TAIL - 3), (0, LANES - ids.shape[0])))


def local(vectors, tiles, tile_rows, tile_cols, row_counts, live_tiles):
    vec_count, seg_len = vectors.shape
    slots, tile_len = tiles.shape[:2]
    rows, cols = lax.axis_size("row"), lax.axis_size("col")
    per_piece = seg_len // tile_len
    row, col = lax.axis_index("row"), lax.axis_index("col")
    grid = (rows, cols)
    join = functools.partial(jnp.concatenate, axis=0)

    live = jnp.arange(slots, dtype=jnp.int32) < live_tiles[0]
    counts = jnp.where(live, row_counts, 0)
    col_row = tile_cols // (cols * per_piece)
    group = col_row // 4 - row // 4
    other = (col_row % 4) ^ (row % 4)
    col_part = (other & 1) * 5 + jnp.where(group == 2, 4, (other >> 1) + 2 * group)
    col_places = col_part * per_piece + tile_cols % per_piece
    tail = tail_of(jnp.where(live, tile_cols, -1))

    rounded = vectors.astype(jnp.bfloat16).reshape(vec_count, per_piece, tile_len).transpose(1, 0, 2).reshape(-1, tile_len)
    place = jnp.stack([col, row * cols * per_piece, (row * cols + col) * per_piece])
    wanted, row_places = requests(place, tile_rows, live_tiles, cols, per_piece)
    across = across_halves(rounded, *grid)
    asked = lax.all_to_all(wanted, "col", 0, 0)
    most = jnp.max(asked[:, 1, 0])
    reply, late_reply, own_reply = replies(place, asked, rounded, cols, slots)
    both = join([rounded, after(across, reply)])
    groups = next_groups(both, *grid, -1)
    reply = over_columns(reply, cols)
    late_reply = lax.cond(most > SHARE, lambda v: over_columns(v, cols), lambda v: v, late_reply)
    here = join([both, *groups])
    there = other_core(here, *grid)
    mirror = mirror_products(row_places, counts, after(reply, here), late_reply, own_reply, tiles, tail)
    mirror_across = across_halves(mirror, *grid)
    there = after(there, mirror)
    forward, late_forward, own_forward = forward_products(col_places, row_places, counts, here, there, tiles, cols)
    mirror_both = join([mirror, after(mirror_across, forward)])
    mirror_groups = next_groups(mirror_both, *grid, 1)
    forward = over_columns(forward, cols)
    late_forward = lax.cond(most > SHARE, lambda v: over_columns(v, cols), lambda v: v, late_forward)
    mirror_here = after(join([mirror_both, *mirror_groups]), late_forward, forward)
    mirror_there = other_core(mirror_here, *grid)
    partial = first_sum(
        place, most.reshape(1), asked, forward, late_forward, own_forward, mirror_here, slots, cols, per_piece
    )
    total = last_sum(place, partial, mirror_there, slots)
    return total.reshape(per_piece, vec_count, tile_len).transpose(1, 0, 2).reshape(vec_count, seg_len)


def solution(mesh):
    placed = (
        P(None, AXES),
        P(AXES, None, None),
        P(AXES),
        P(AXES),
        P(AXES),
        P(AXES),
    )
    return jax.shard_map(local, mesh=mesh, in_specs=placed, out_specs=P(None, AXES), check_vma=False)
```
